32 devices in a mesh: group: 1, expert: 32 (over z, y, x, core), hslice: 1.
Axes of the slice: x: 2, y: 2, z: 4, core: 2. Of those that a mesh axis runs over, the one named last changes fastest.
Arguments:
- tokens: bfloat16 [2048, 3584], P(('group', 'expert')), may hold values from -6 to 6
- routes: int32 [2048, 8], P(('group', 'expert')), may hold values from 0 to 15, all different within a row; in each aligned block of 64 rows (0 to 63, 64 to 127, ...) at most 36 rows name the same one
- gate_values: float32 [2048, 8], P(('group', 'expert')), may hold values from 0.1 to 1
- gate_up: bfloat16 [32, 3584, 2, 512], P('expert', None, None, 'hslice'), may hold values from -0.09375 to 0.09375
- down_weight: bfloat16 [32, 512, 3584], P('expert', None, 'hslice'), may hold values from -0.1875 to 0.1875
Outputs:
- mixed_out: bfloat16 [2048, 3584], P(('group', 'expert'), 'hslice')
The draws below stay inside these ranges and needn't reach their ends.
Inputs may be any that keep to these rules, and one draw needn't show every extreme that they name: `routes`: each row names 8 different experts. Within the rows of one index of expert (aligned blocks of 64 tokens) no expert is named more than 36 times, a bound that some block reaches.
All inputs are finite; a program needn't handle non-finite values.
Results may differ from the reference program's by a relative error of at most 0.0065.
Values may be sent and summed in bfloat16 or wider, within the bound.
A program may use at most 64 MiB of HBM per device.

```python
import math
import jax
import jax.numpy as jnp
import numpy as np
from jax import lax

D = 3584
FF = 1024
TOK_DEV = 64
EXPERTS = 16
TOPK = 8
CAP = 36
TOKENS = 2048
N_EXPERT = 32


def level_of(rng, extent, pieces, low, high):
    gain, own = 1.0, jax.random.fold_in(rng, 6)
    for dim, shards_of in pieces:
        heights = jnp.exp(jax.random.uniform(jax.random.fold_in(own, dim), (shards_of,), jnp.float32, low / len(pieces), high / len(pieces)))
        gain = gain * jnp.repeat(heights, extent[dim] // shards_of).reshape([-1 if axis == dim else 1 for axis in range(len(extent))])
    return gain


def shared_out(own_key, own, number, rows, amount, top, reach, skew):
    sequence = jax.random.permutation(own_key, amount)
    crowded, common = portions_of(amount, rows * top, reach, skew, True), portions_of(amount, rows * top, reach, skew, False)
    places = jnp.arange(amount)

    def named(sizes, rotation):
        used = int((sizes > 0).sum())
        fixed = max(1, used // 4)
        passed = fixed + (places - fixed + rotation * (used - fixed)) % max(1, amount - fixed)
        return jnp.zeros((amount,), jnp.int32).at[sequence[jnp.where(places < fixed, places, passed)]].set(jnp.asarray(sizes, jnp.int32))

    sizes = jnp.where(number % 4 == 0, named(crowded, number // 4), named(common, number - number // 4 - 1))
    mixed = jax.random.permutation(jax.random.fold_in(own, 3), amount)
    source_of, sink = mixed[0:amount // 2 * 2:2], mixed[1:amount // 2 * 2:2]
    room = jnp.minimum(sizes[source_of] - 1, reach - sizes[sink]) // 2
    room = jnp.where((source_of == sequence[0]) | (sink == sequence[0]) | (sizes[sink] == 0), 0, jnp.maximum(room, 0))
    passed = jax.random.randint(jax.random.fold_in(own, 4), (amount // 2,), 0, 1 << 20) % (room + 1)
    sizes = sizes.at[source_of].add(-passed).at[sink].add(passed)
    members = jnp.searchsorted(jnp.cumsum(sizes), jnp.arange(rows * top), side="right").astype(jnp.int32)
    listing = members.reshape(top, rows).T
    listing = listing[jax.random.permutation(jax.random.fold_in(own, 1), rows)]
    rotation = jax.random.randint(jax.random.fold_in(own, 2), (rows, 1), 0, top)
    return jnp.take_along_axis(listing, (jnp.arange(top)[None, :] + rotation) % top, axis=1)


def portions_of(amount, total, most, skew, full):
    portions = [(1 << 20) // math.isqrt(standing ** skew) + 1 for standing in range(1, amount + 1)]
    largest = most if full else min(most, max(-(-total // amount), total * portions[0] // sum(portions)))
    least = 1 if total - largest >= amount - 1 else 0
    given, surplus = [largest] + [least] * (amount - 1), total - largest - least * (amount - 1)
    while surplus > 0:
        free = [i for i in range(1, amount) if given[i] < largest] or [i for i in range(1, amount) if given[i] < most]
        mass, remaining = sum([portions[i] for i in free]), surplus
        for i in free:
            addition = min(most - given[i], max(1, remaining * portions[i] // mass), surplus)
            given[i] = given[i] + addition
            surplus = surplus - addition
    return np.array(given)


def bell_draw(key, dims, width, reach, split=(), kind=jnp.bfloat16):
    loudness = level_of(key, dims, split, -0.22, 0.18) if split else 1.0
    result = jax.random.normal(key, dims, jnp.float32) * width * loudness
    return jnp.minimum(jnp.maximum(result, -reach), reach).astype(kind)


def setup_inputs(seed: int = 0, part: int = 0) -> dict:
    key_of = jax.random.split(jax.random.key(seed), 6)
    part_keys = jax.random.split(jax.random.fold_in(key_of[5], part), 6)
    tokens = bell_draw(part_keys[0], (TOKENS, D), 1.0, 6.0, ((0, 32),))
    routes_keys = jax.random.split(jax.random.fold_in(part_keys[1], 1), TOKENS // TOK_DEV)
    routes_turns = jax.random.permutation(jax.random.fold_in(part_keys[1], 3), TOKENS // TOK_DEV)
    routes = jax.vmap(lambda own, number: shared_out(jax.random.fold_in(part_keys[1], 2), own, number, TOK_DEV, EXPERTS, TOPK, CAP, 2))(routes_keys, routes_turns).reshape((TOKENS, TOPK))
    gate_values = jnp.clip(0.1 + 0.9 * jax.random.uniform(part_keys[2], (TOKENS, TOPK), jnp.float32) ** level_of(part_keys[2], (TOKENS, TOPK), ((0, 32),), -0.2, 0.2), 0.1, 1.0)
    gate_up = bell_draw(key_of[3], (2 * EXPERTS, D, 2, FF // 2), D ** -0.5, 0.09375, ((0, 32),))
    down_weight = bell_draw(key_of[4], (2 * EXPERTS, FF // 2, D), FF ** -0.5, 0.1875, ((0, 32),))
    return {"tokens": tokens, "routes": routes, "gate_values": gate_values, "gate_up": gate_up, "down_weight": down_weight}


def reference(tokens, routes, gate_values, gate_up, down_weight):
    expert_ids = routes.reshape(-1).astype(jnp.int32)
    member = (expert_ids[:, None] == jnp.arange(EXPERTS, dtype=jnp.int32)[None, :]).astype(jnp.int32)
    blocks = member.reshape(N_EXPERT, TOK_DEV * TOPK, EXPERTS)
    before = (jnp.cumsum(blocks, axis=1) - blocks).astype(jnp.int32)
    position = jnp.sum(before * blocks, axis=2).astype(jnp.int32).reshape(-1)
    source = jnp.arange(TOKENS * TOPK, dtype=jnp.int32) // (TOK_DEV * TOPK)
    token_row = jnp.arange(TOKENS * TOPK, dtype=jnp.int32) // TOPK
    slot_table = jnp.zeros((EXPERTS, N_EXPERT, CAP), jnp.int32).at[expert_ids, source, position].set(token_row)
    half_units = FF // 2

    def one_expert(expert_index):
        inputs = jnp.take(tokens, slot_table[expert_index].reshape(-1), axis=0)
        weight_pair = lax.dynamic_slice_in_dim(gate_up, 2 * expert_index, 2, 0)
        gate_matrix = jnp.transpose(weight_pair[:, :, 0, :], (1, 0, 2)).reshape(D, FF)
        up_matrix = jnp.transpose(weight_pair[:, :, 1, :], (1, 0, 2)).reshape(D, FF)
        down_matrix = lax.dynamic_slice_in_dim(down_weight, 2 * expert_index, 2, 0).reshape(FF, D)
        gate_value = jnp.dot(inputs, gate_matrix, preferred_element_type=jnp.float32)
        up_value = jnp.dot(inputs, up_matrix, preferred_element_type=jnp.float32)
        hidden = (jax.nn.silu(gate_value) * up_value).astype(jnp.bfloat16)
        summed = jnp.zeros((N_EXPERT * CAP, D), jnp.float32)
        for segment in range(2):
            offset = segment * half_units
            partial_value = jnp.dot(hidden[:, offset:offset + half_units], down_matrix[offset:offset + half_units], preferred_element_type=jnp.float32)
            partial_value = lax.optimization_barrier(partial_value.astype(jnp.bfloat16))
            summed = summed + partial_value.astype(jnp.float32)
        return lax.optimization_barrier(summed.astype(jnp.bfloat16))

    outputs = lax.map(one_expert, jnp.arange(EXPERTS, dtype=jnp.int32))
    flat_index = ((expert_ids * N_EXPERT + source) * CAP + position).astype(jnp.int32)
    picked = jnp.take(outputs.reshape(EXPERTS * N_EXPERT * CAP, D), flat_index, axis=0).astype(jnp.float32)
    mixed_out = jnp.sum(picked.reshape(TOKENS, TOPK, D) * gate_values[:, :, None], axis=1)
    return mixed_out.astype(jnp.bfloat16)
```

```python
import functools

import jax
import jax.numpy as jnp
from jax import lax
from jax.experimental import pallas as pl
from jax.experimental.pallas import tpu as pltpu
from jax.sharding import PartitionSpec as P

MESH = pl.DeviceIdType.MESH
F32 = jnp.float32
BF16 = jnp.bfloat16


def capacity_of(tok_count, choices, experts):
    return min(tok_count, 2 * ((9 * tok_count * choices + 16 * experts - 1) // (16 * experts)))


def chunks_of(features):
    for count in (7, 4, 2):
        if features % (count * 128) == 0:
            return count
    return 1


def fused_kernel(
    planes, cap, chunks,
    tokens, routes, gates, gate_up, down,
    out,
    info, line, pack_hot, mix_hi, mix_lo, rows_out, rows_in, acc, hidden,
    w_up, w_down, y_out, y_in, part, part_own, part_in,
    i_s, i_r, z_s, z_r, x_s, x_r, y_s, y_r, p_s, p_r, wl, ws, wr, dl, ds, dr,
):
    me = lax.axis_index("expert")
    core = lax.rem(me, 2)
    x = lax.rem(me // 2, 2)
    y = lax.rem(me // 4, 2)
    z = me // 8
    tok = tokens.shape[0]
    width = tokens.shape[1] // chunks
    half = gate_up.shape[2]
    group = planes * cap
    partner = me + 1 - 2 * core

    def z_peer(d):
        return lax.rem(z + d, planes) * 8 + y * 4 + x * 2 + core

    def plane_xy(r):
        px = x if r % 2 == 0 else 1 - x
        py = y if r // 2 == 0 else 1 - y
        return py, px

    def xy_peer(r):
        py, px = plane_xy(r)
        return z * 8 + py * 4 + px * 2 + core

    def remote(src, dst, s, r, device):
        return pltpu.make_async_remote_copy(
            src_ref=src, dst_ref=dst, send_sem=s, recv_sem=r,
            device_id={"expert": device}, device_id_type=MESH)

    def columns(j):
        return pl.ds(pl.multiple_of(j * width, 128), width)

    own_rows = pl.ds(pl.multiple_of(z * tok, 16), tok)

    def up_local(j):
        return pltpu.make_async_copy(
            gate_up.at[:, pl.ds(j * width, width)], w_up.at[0, :, pl.ds(j * width, width)], wl.at[j])

    def up_swap(j):
        return remote(gate_up.at[:, pl.ds(j * width, width)],
                      w_up.at[1, :, pl.ds(j * width, width)], ws.at[j], wr.at[j], partner)

    down_local = pltpu.make_async_copy(down, w_down.at[pl.ds(0, half)], dl)
    down_swap = remote(down, w_down.at[pl.ds(half, half)], ds, dr, partner)

    def info_send(d):
        return remote(info.at[z], info.at[z], i_s.at[d - 1], i_r.at[d - 1], z_peer(d))

    def z_send(d, j):
        return remote(tokens.at[:, columns(j)], line.at[j, own_rows],
                      z_s.at[d - 1, j], z_r.at[d - 1, j], z_peer(d))

    def x_send(r, j):
        return remote(rows_out.at[j, pl.ds((r - 1) * group, group)],
                      rows_in.at[j, pl.ds(r * group, group)],
                      x_s.at[r - 1, j], x_r.at[r - 1, j], xy_peer(r))

    def y_send(r, j):
        return remote(y_out.at[j, pl.ds((r - 1) * group, group)],
                      y_in.at[j, pl.ds(r * group, group)],
                      y_s.at[r - 1, j], y_r.at[r - 1, j], xy_peer(r))

    def p_send(d, j):
        there = pl.ds(pl.multiple_of(lax.rem(z + d, planes) * tok, 16), tok)
        return remote(part.at[j, there], part_in.at[j, d - 1],
                      p_s.at[d - 1, j], p_r.at[d - 1, j], z_peer(d))

    def each_chunk(body):
        def step(j, carry):
            body(j)
            return carry
        lax.fori_loop(0, chunks, step, 0)

    each_chunk(lambda j: up_local(j).start())
    down_local.start()

    lane = lax.broadcasted_iota(jnp.int32, (tok, 128), 1)
    weight = jnp.zeros((tok, 128), F32)
    for k in range(routes.shape[1]):
        weight = weight + jnp.where(routes[:, k:k + 1] == lane, gates[:, k:k + 1], 0.0)
    member = jnp.where(weight > 0.0, 1.0, 0.0)
    lower = jnp.where(
        lax.broadcasted_iota(jnp.int32, (tok, tok), 1) < lax.broadcasted_iota(jnp.int32, (tok, tok), 0),
        1.0, 0.0).astype(BF16)
    rank = jnp.dot(lower, member.astype(BF16), preferred_element_type=F32)
    slot = jnp.where(weight > 0.0, rank + (z * cap).astype(F32), -10000.0)
    info[z, :, 0:128] = weight
    info[z, :, 128:256] = slot

    barrier = pltpu.get_barrier_semaphore()
    peers = [z_peer(d) for d in range(1, planes)] + [xy_peer(r) for r in (1, 2, 3)] + [partner]
    for peer in peers:
        pl.semaphore_signal(barrier, inc=1, device_id={"expert": peer}, device_id_type=MESH)
    pl.semaphore_wait(barrier, len(peers))

    for d in range(1, planes):
        info_send(d).start()

    def start_z(j):
        for d in range(1, planes):
            z_send(d, j).start()
    each_chunk(start_z)
    each_chunk(lambda j: up_swap(j).start())
    down_swap.start()

    def own_line(j):
        line[j, own_rows, :] = tokens[:, columns(j)]
    each_chunk(own_line)

    for d in range(1, planes):
        info_send(d).wait_recv()

    total = planes * tok
    info_all = info[...].reshape(total, 256)
    weights = info_all[:, 0:128]
    slots = info_all[:, 128:256]
    slots_t = jnp.transpose(slots)
    row_id = lax.broadcasted_iota(jnp.int32, (128, total), 0)
    col_id = lax.broadcasted_iota(jnp.int32, (total, 128), 1)
    pack = jnp.zeros((4 * group, total), F32)
    mix = jnp.zeros((total, 4 * group), F32)
    pack_at = lax.broadcasted_iota(jnp.int32, (4 * group, total), 0).astype(F32)
    mix_at = lax.broadcasted_iota(jnp.int32, (total, 4 * group), 1).astype(F32)
    for r in range(4):
        py, px = plane_xy(r)
        expert = z * 4 + py * 2 + px
        slot_row = jnp.sum(jnp.where(row_id == expert, slots_t, 0.0), axis=0, keepdims=True)
        slot_col = jnp.sum(jnp.where(col_id == expert, slots, 0.0), axis=1, keepdims=True)
        weight_col = jnp.sum(jnp.where(col_id == expert, weights, 0.0), axis=1, keepdims=True)
        pack = pack + jnp.where(pack_at == slot_row + float(r * group), 1.0, 0.0)
        mix = mix + jnp.where(mix_at == slot_col + float(r * group), weight_col, 0.0)
    pack_hot[...] = pack.astype(BF16)
    high = mix.astype(BF16)
    mix_hi[...] = high
    mix_lo[...] = (mix - high.astype(F32)).astype(BF16)

    def pack_step(j):
        for d in range(1, planes):
            z_send(d, j).wait_recv()
        packed = jnp.dot(pack_hot[...], line[j], preferred_element_type=F32).astype(BF16)
        rows_out[j] = packed[group:]
        for r in (3, 1, 2):
            x_send(r, j).start()
        rows_in[j, 0:group, :] = packed[0:group]
    each_chunk(pack_step)

    def up_step(j):
        for r in (1, 2, 3):
            x_send(r, j).wait_recv()
        up_local(j).wait()
        up_swap(j).wait_recv()

        def tile(n, carry):
            h, g = n // 2, lax.rem(n, 2)
            term = jnp.dot(rows_in[j], w_up[h, g, pl.ds(j * width, width), :],
                           preferred_element_type=F32)

            @pl.when(j == 0)
            def _():
                acc[n] = term

            @pl.when(j > 0)
            def _():
                acc[n] = acc[n] + term
            return carry
        lax.fori_loop(0, 4, tile, 0)
    each_chunk(up_step)

    for h in range(2):
        gate = acc[2 * h]
        hidden[:, h * half:(h + 1) * half] = (gate / (1.0 + jnp.exp(-gate)) * acc[2 * h + 1]).astype(BF16)

    down_local.wait()
    down_swap.wait_recv()

    def down_step(j):
        result = jnp.dot(hidden[...], w_down[:, columns(j)], preferred_element_type=F32).astype(BF16)
        y_out[j] = result[group:]
        for r in (3, 1, 2):
            y_send(r, j).start()
        y_in[j, 0:group, :] = result[0:group]
    each_chunk(down_step)

    def mix_step(j):
        for r in (1, 2, 3):
            y_send(r, j).wait_recv()
        rows = y_in[j]
        part_own[j] = (jnp.dot(mix_hi[...], rows, preferred_element_type=F32)
                       + jnp.dot(mix_lo[...], rows, preferred_element_type=F32))
        part[j] = part_own[j].astype(BF16)
        for d in range(1, planes):
            p_send(d, j).start()
    each_chunk(mix_step)

    def last_step(j):
        for d in range(1, planes):
            p_send(d, j).wait_recv()
        value = part_own[j, own_rows, :]
        for d in range(1, planes):
            value = value + part_in[j, d - 1].astype(F32)
        out[:, columns(j)] = value.astype(BF16)
    each_chunk(last_step)

    for d in range(1, planes):
        info_send(d).wait_send()

    def drain(j):
        for d in range(1, planes):
            z_send(d, j).wait_send()
            p_send(d, j).wait_send()
        for r in (1, 2, 3):
            x_send(r, j).wait_send()
            y_send(r, j).wait_send()
        up_swap(j).wait_send()
    each_chunk(drain)
    down_swap.wait_send()


def fused(tokens, routes, gate_values, gate_up, down_weight):
    devices = lax.axis_size("expert")
    planes = devices // 8
    tok, choices = routes.shape
    features = tokens.shape[1]
    half = gate_up.shape[3]
    cap = capacity_of(tok, choices, devices // 2)
    chunks = chunks_of(features)
    width = features // chunks
    group = planes * cap
    total = planes * tok
    up = jnp.transpose(gate_up.reshape(features, 2, half), (1, 0, 2))
    down = down_weight.reshape(half, features)
    dma = pltpu.SemaphoreType.DMA
    vmem = pltpu.VMEM
    pairs = lambda n: [dma((n, chunks)), dma((n, chunks))]
    return pl.pallas_call(
        functools.partial(fused_kernel, planes, cap, chunks),
        out_shape=jax.ShapeDtypeStruct((tok, features), BF16),
        in_specs=[pl.BlockSpec(memory_space=pltpu.VMEM)] * 3 + [pl.BlockSpec(memory_space=pl.ANY)] * 2,
        out_specs=pl.BlockSpec(memory_space=pltpu.VMEM),
        scratch_shapes=[
            vmem((planes, tok, 256), F32),
            vmem((chunks, total, width), BF16),
            vmem((4 * group, total), BF16),
            vmem((total, 4 * group), BF16),
            vmem((total, 4 * group), BF16),
            vmem((chunks, 3 * group, width), BF16),
            vmem((chunks, 4 * group, width), BF16),
            vmem((4, 4 * group, half), F32),
            vmem((4 * group, 2 * half), BF16),
            vmem((2, 2, features, half), BF16),
            vmem((2 * half, features), BF16),
            vmem((chunks, 3 * group, width), BF16),
            vmem((chunks, 4 * group, width), BF16),
            vmem((chunks, total, width), BF16),
            vmem((chunks, total, width), F32),
            vmem((chunks, planes - 1, tok, width), BF16),
            dma((planes - 1,)), dma((planes - 1,)),
            *pairs(planes - 1), *pairs(3), *pairs(3), *pairs(planes - 1),
            dma((chunks,)), dma((chunks,)), dma((chunks,)), dma, dma, dma,
        ],
        compiler_params=pltpu.CompilerParams(
            collective_id=0, has_side_effects=True, vmem_limit_bytes=62 * 1024 * 1024),
    )(tokens, routes, gate_values, up, down)


def partner_2(block, axis, distance):
    count = lax.axis_size(axis)
    route = []
    for low in range(count):
        high = low | 1 << distance
        if high != low and high < count:
            route += [(low, high), (high, low)]
    return lax.ppermute(block, axis, route)


def swiglu_rows(inputs, weights, split_at):
    both_parts = jnp.dot(inputs, weights, preferred_element_type=jnp.float32)
    return (jax.nn.silu(both_parts[:, :split_at]) * both_parts[:, split_at:]).astype(jnp.bfloat16)


def down_fold(down_matrix, hidden_piece):
    return jnp.dot(hidden_piece, down_matrix, preferred_element_type=jnp.float32)


def local(tokens, routes, gate_values, gate_up, down_weight):
    devices = lax.axis_size("expert")
    experts = devices // 2
    tok_count, choices = routes.shape
    features = tokens.shape[1]
    hidden_width = gate_up.shape[3]
    half_units = down_weight.shape[1]
    columns = down_weight.shape[2]
    capacity = capacity_of(tok_count, choices, experts)
    slot_rows = capacity // 2
    targets = experts * capacity
    expert_ids = routes.reshape(-1)
    member = (expert_ids[:, None] == jnp.arange(experts, dtype=jnp.int32)[None, :]).astype(
        jnp.int32
    )
    earlier = jnp.sum((jnp.cumsum(member, axis=0) - member) * member, axis=1)
    target = expert_ids * capacity + earlier
    target_hot = (target[:, None] == jnp.arange(targets, dtype=jnp.int32)[None, :]).astype(
        jnp.bfloat16
    )
    repeated = jnp.broadcast_to(tokens[:, None, :], (tok_count, choices, features)).reshape(
        tok_count * choices, features
    )
    outgoing = lax.dot_general(
        target_hot, repeated, (((0,), (0,)), ((), ())), preferred_element_type=jnp.float32
    ).astype(jnp.bfloat16)
    own_half = lax.axis_index("expert") % 2
    doubled = jnp.broadcast_to(
        outgoing.reshape(experts, 1, capacity, features), (experts, 2, capacity, features)
    )
    arrived = lax.all_to_all(
        doubled.reshape(devices * capacity, features),
        "expert",
        split_axis=0,
        concat_axis=0,
        tiled=True,
    )
    own_gate_up = gate_up.reshape(features, 2 * hidden_width)
    own_down = down_weight.reshape(half_units, columns)
    hidden_all = swiglu_rows(arrived, own_gate_up, hidden_width)
    summed = down_fold(own_down, lax.all_gather(hidden_all, "hslice", axis=1, tiled=True))
    summed = summed.astype(jnp.bfloat16)
    partner = partner_2(summed, "expert", 0)
    pair_total = (
        (summed.astype(jnp.float32) + partner.astype(jnp.float32))
        .astype(jnp.bfloat16)
        .reshape(devices, 2, slot_rows, columns)
    )
    kept_slot = jnp.where(own_half == 0, pair_total[:, 0], pair_total[:, 1]).reshape(
        devices * slot_rows, columns
    )
    merged = lax.all_to_all(kept_slot, "expert", split_axis=0, concat_axis=0, tiled=True)
    merged = merged.astype(jnp.float32)
    weights_map = (target_hot.astype(jnp.float32) * gate_values.reshape(-1)[:, None]).reshape(
        tok_count, choices, targets
    )
    weights_map = jnp.sum(weights_map, axis=1)
    mixed_out = jnp.dot(
        weights_map, merged, precision=lax.Precision.HIGHEST, preferred_element_type=jnp.float32
    )
    return mixed_out.astype(jnp.bfloat16)


def local_any(tokens, routes, gate_values, gate_up, down_weight):
    devices = lax.axis_size("expert")
    tok, choices = routes.shape
    planes = devices // 8
    fits = (
        lax.axis_size("hslice") == 1
        and devices % 8 == 0
        and planes in (2, 4)
        and devices // 2 <= 128
        and tok % 16 == 0
        and planes * capacity_of(tok, choices, devices // 2) % 16 == 0
        and tokens.shape[1] % 128 == 0
        and gate_up.shape[3] % 128 == 0
    )
    call = fused if fits else local
    return call(tokens, routes, gate_values, gate_up, down_weight)


def solution(mesh):
    in_specs = (
        P(("group", "expert"), None),
        P(("group", "expert"), None),
        P(("group", "expert"), None),
        P("expert", None, None, "hslice"),
        P("expert", None, "hslice"),
    )
    out_specs = P(("group", "expert"), "hslice")
    return jax.shard_map(local_any, mesh=mesh, in_specs=in_specs, out_specs=out_specs, check_vma=False)
```

```python
import functools

import jax
import jax.numpy as jnp
from jax import lax
from jax.experimental import pallas as pl
from jax.experimental.pallas import tpu as pltpu
from jax.sharding import PartitionSpec as P

MESH = pl.DeviceIdType.MESH
F32 = jnp.float32
BF16 = jnp.bfloat16


def capacity_of(tok_count, choices, experts):
    return min(tok_count, 2 * ((9 * tok_count * choices + 16 * experts - 1) // (16 * experts)))


def chunks_of(features):
    for count in (7, 4, 2):
        if features % (count * 128) == 0:
            return count
    return 1


def fused_kernel(
    planes, cap, chunks,
    tokens, routes, gates, gate_up, down,
    out,
    info, line, pack_hot, mix_hi, mix_lo, rows_out, rows_in, acc, hidden,
    w_raw, w_up, w_down, y_out, y_in, part, part_own, part_in,
    i_s, i_r, z_s, z_r, x_s, x_r, y_s, y_r, p_s, p_r, wl, ws, wr, dl, ds, dr,
):
    me = lax.axis_index("expert")
    core = lax.rem(me, 2)
    x = lax.rem(me // 2, 2)
    y = lax.rem(me // 4, 2)
    z = me // 8
    tok = tokens.shape[0]
    width = tokens.shape[1] // chunks
    half = gate_up.shape[2]
    group = planes * cap
    partner = me + 1 - 2 * core

    def z_peer(d):
        return lax.rem(z + d, planes) * 8 + y * 4 + x * 2 + core

    def plane_xy(r):
        px = x if r % 2 == 0 else 1 - x
        py = y if r // 2 == 0 else 1 - y
        return py, px

    def xy_peer(r):
        py, px = plane_xy(r)
        return z * 8 + py * 4 + px * 2 + core

    def remote(src, dst, s, r, device):
        return pltpu.make_async_remote_copy(
            src_ref=src, dst_ref=dst, send_sem=s, recv_sem=r,
            device_id={"expert": device}, device_id_type=MESH)

    def columns(j):
        return pl.ds(pl.multiple_of(j * width, 128), width)

    own_rows = pl.ds(pl.multiple_of(z * tok, 16), tok)

    def up_local(j):
        return pltpu.make_async_copy(
            gate_up.at[pl.ds(j * width, width)], w_raw.at[pl.ds(j * width, width)], wl.at[j])

    def up_swap(j):
        return remote(w_up.at[0, :, pl.ds(j * width, width)],
                      w_up.at[1, :, pl.ds(j * width, width)], ws.at[j], wr.at[j], partner)

    down_local = pltpu.make_async_copy(down, w_down.at[pl.ds(0, half)], dl)
    down_swap = remote(down, w_down.at[pl.ds(half, half)], ds, dr, partner)

    def info_send(d):
        return remote(info.at[z], info.at[z], i_s.at[d - 1], i_r.at[d - 1], z_peer(d))

    def z_send(d, j):
        return remote(tokens.at[:, columns(j)], line.at[j, own_rows],
                      z_s.at[d - 1, j], z_r.at[d - 1, j], z_peer(d))

    def x_send(r, j):
        return remote(rows_out.at[j, pl.ds((r - 1) * group, group)],
                      rows_in.at[j, pl.ds(r * group, group)],
                      x_s.at[r - 1, j], x_r.at[r - 1, j], xy_peer(r))

    def y_send(r, j):
        return remote(y_out.at[j, pl.ds((r - 1) * group, group)],
                      y_in.at[j, pl.ds(r * group, group)],
                      y_s.at[r - 1, j], y_r.at[r - 1, j], xy_peer(r))

    def p_send(d, j):
        there = pl.ds(pl.multiple_of(lax.rem(z + d, planes) * tok, 16), tok)
        return remote(part.at[j, there], part_in.at[j, d - 1],
                      p_s.at[d - 1, j], p_r.at[d - 1, j], z_peer(d))

    def each_chunk(body):
        def step(j, carry):
            body(j)
            return carry
        lax.fori_loop(0, chunks, step, 0)

    each_chunk(lambda j: up_local(j).start())
    down_local.start()

    expert_row = lax.broadcasted_iota(jnp.int32, (128, tok), 0)
    weight_t = jnp.zeros((128, tok), F32)
    for k in range(routes.shape[0]):
        weight_t = weight_t + jnp.where(routes[k:k + 1, :] == expert_row, gates[k:k + 1, :], 0.0)
    weight = jnp.transpose(weight_t)
    member = jnp.where(weight > 0.0, 1.0, 0.0)
    lower = jnp.where(
        lax.broadcasted_iota(jnp.int32, (tok, tok), 1) < lax.broadcasted_iota(jnp.int32, (tok, tok), 0),
        1.0, 0.0).astype(BF16)
    rank = jnp.dot(lower, member.astype(BF16), preferred_element_type=F32)
    slot = jnp.where(weight > 0.0, rank + (z * cap).astype(F32), -10000.0)
    info[z, :, 0:128] = weight
    info[z, :, 128:256] = slot

    barrier = pltpu.get_barrier_semaphore()
    peers = [z_peer(d) for d in range(1, planes)] + [xy_peer(r) for r in (1, 2, 3)] + [partner]
    for peer in peers:
        pl.semaphore_signal(barrier, inc=1, device_id={"expert": peer}, device_id_type=MESH)
    pl.semaphore_wait(barrier, len(peers))

    for d in range(1, planes):
        info_send(d).start()

    def start_z(j):
        for d in range(1, planes):
            z_send(d, j).start()
    each_chunk(start_z)
    down_swap.start()

    def own_line(j):
        line[j, own_rows, :] = tokens[:, columns(j)]
    each_chunk(own_line)

    for d in range(1, planes):
        info_send(d).wait_recv()

    total = planes * tok
    info_all = info[...].reshape(total, 256)
    weights = info_all[:, 0:128]
    slots = info_all[:, 128:256]
    slots_t = jnp.transpose(slots)
    row_id = lax.broadcasted_iota(jnp.int32, (128, total), 0)
    col_id = lax.broadcasted_iota(jnp.int32, (total, 128), 1)
    pack = jnp.zeros((4 * group, total), F32)
    mix = jnp.zeros((total, 4 * group), F32)
    pack_at = lax.broadcasted_iota(jnp.int32, (4 * group, total), 0).astype(F32)
    mix_at = lax.broadcasted_iota(jnp.int32, (total, 4 * group), 1).astype(F32)
    for r in range(4):
        py, px = plane_xy(r)
        expert = z * 4 + py * 2 + px
        slot_row = jnp.sum(jnp.where(row_id == expert, slots_t, 0.0), axis=0, keepdims=True)
        slot_col = jnp.sum(jnp.where(col_id == expert, slots, 0.0), axis=1, keepdims=True)
        weight_col = jnp.sum(jnp.where(col_id == expert, weights, 0.0), axis=1, keepdims=True)
        pack = pack + jnp.where(pack_at == slot_row + float(r * group), 1.0, 0.0)
        mix = mix + jnp.where(mix_at == slot_col + float(r * group), weight_col, 0.0)
    pack_hot[...] = pack.astype(BF16)
    high = mix.astype(BF16)
    mix_hi[...] = high
    mix_lo[...] = (mix - high.astype(F32)).astype(BF16)

    def pack_step(j):
        for d in range(1, planes):
            z_send(d, j).wait_recv()
        packed = jnp.dot(pack_hot[...], line[j], preferred_element_type=F32).astype(BF16)
        rows_out[j] = packed[group:]
        for r in (3, 1, 2):
            x_send(r, j).start()
        rows_in[j, 0:group, :] = packed[0:group]

        up_local(j).wait()

        def split(n, carry):
            rows = pl.ds(pl.multiple_of(j * width + n * 32, 32), 32)
            w_up[0, 0, rows, :] = w_raw[rows, 0, :]
            w_up[0, 1, rows, :] = w_raw[rows, 1, :]
            return carry
        lax.fori_loop(0, width // 32, split, 0)
        up_swap(j).start()
    each_chunk(pack_step)

    def up_step(j):
        for r in (1, 2, 3):
            x_send(r, j).wait_recv()
        up_swap(j).wait_recv()

        def tile(n, carry):
            h, g = n // 2, lax.rem(n, 2)
            term = jnp.dot(rows_in[j], w_up[h, g, pl.ds(j * width, width), :],
                           preferred_element_type=F32)

            @pl.when(j == 0)
            def _():
                acc[n] = term

            @pl.when(j > 0)
            def _():
                acc[n] = acc[n] + term
            return carry
        lax.fori_loop(0, 4, tile, 0)
    each_chunk(up_step)

    for h in range(2):
        gate = acc[2 * h]
        hidden[:, h * half:(h + 1) * half] = (gate / (1.0 + jnp.exp(-gate)) * acc[2 * h + 1]).astype(BF16)

    down_local.wait()
    down_swap.wait_recv()

    def down_step(j):
        result = jnp.dot(hidden[...], w_down[:, columns(j)], preferred_element_type=F32).astype(BF16)
        y_out[j] = result[group:]
        for r in (3, 1, 2):
            y_send(r, j).start()
        y_in[j, 0:group, :] = result[0:group]
    each_chunk(down_step)

    def mix_step(j):
        for r in (1, 2, 3):
            y_send(r, j).wait_recv()
        rows = y_in[j]
        part_own[j] = (jnp.dot(mix_hi[...], rows, preferred_element_type=F32)
                       + jnp.dot(mix_lo[...], rows, preferred_element_type=F32))
        part[j] = part_own[j].astype(BF16)
        for d in range(1, planes):
            p_send(d, j).start()
    each_chunk(mix_step)

    def last_step(j):
        for d in range(1, planes):
            p_send(d, j).wait_recv()
        value = part_own[j, own_rows, :]
        for d in range(1, planes):
            value = value + part_in[j, d - 1].astype(F32)
        out[:, columns(j)] = value.astype(BF16)
    each_chunk(last_step)

    for d in range(1, planes):
        info_send(d).wait_send()

    def drain(j):
        for d in range(1, planes):
            z_send(d, j).wait_send()
            p_send(d, j).wait_send()
        for r in (1, 2, 3):
            x_send(r, j).wait_send()
            y_send(r, j).wait_send()
        up_swap(j).wait_send()
    each_chunk(drain)
    down_swap.wait_send()


def fused(tokens, routes, gate_values, gate_up, down_weight):
    devices = lax.axis_size("expert")
    planes = devices // 8
    tok, choices = routes.shape
    features = tokens.shape[1]
    half = gate_up.shape[3]
    cap = capacity_of(tok, choices, devices // 2)
    chunks = chunks_of(features)
    width = features // chunks
    group = planes * cap
    total = planes * tok
    up = gate_up.reshape(features, 2, half)
    down = down_weight.reshape(half, features)
    dma = pltpu.SemaphoreType.DMA
    vmem = pltpu.VMEM
    pairs = lambda n: [dma((n, chunks)), dma((n, chunks))]
    return pl.pallas_call(
        functools.partial(fused_kernel, planes, cap, chunks),
        out_shape=jax.ShapeDtypeStruct((tok, features), BF16),
        in_specs=[pl.BlockSpec(memory_space=pltpu.VMEM)] * 3 + [pl.BlockSpec(memory_space=pl.ANY)] * 2,
        out_specs=pl.BlockSpec(memory_space=pltpu.VMEM),
        scratch_shapes=[
            vmem((planes, tok, 256), F32),
            vmem((chunks, total, width), BF16),
            vmem((4 * group, total), BF16),
            vmem((total, 4 * group), BF16),
            vmem((total, 4 * group), BF16),
            vmem((chunks, 3 * group, width), BF16),
            vmem((chunks, 4 * group, width), BF16),
            vmem((4, 4 * group, half), F32),
            vmem((4 * group, 2 * half), BF16),
            vmem((features, 2, half), BF16),
            vmem((2, 2, features, half), BF16),
            vmem((2 * half, features), BF16),
            vmem((chunks, 3 * group, width), BF16),
            vmem((chunks, 4 * group, width), BF16),
            vmem((chunks, total, width), BF16),
            vmem((chunks, total, width), F32),
            vmem((chunks, planes - 1, tok, width), BF16),
            dma((planes - 1,)), dma((planes - 1,)),
            *pairs(planes - 1), *pairs(3), *pairs(3), *pairs(planes - 1),
            dma((chunks,)), dma((chunks,)), dma((chunks,)), dma, dma, dma,
        ],
        compiler_params=pltpu.CompilerParams(
            collective_id=0, has_side_effects=True, vmem_limit_bytes=62 * 1024 * 1024),
    )(tokens, jnp.transpose(routes), jnp.transpose(gate_values), up, down)


def partner_2(block, axis, distance):
    count = lax.axis_size(axis)
    route = []
    for low in range(count):
        high = low | 1 << distance
        if high != low and high < count:
            route += [(low, high), (high, low)]
    return lax.ppermute(block, axis, route)


def swiglu_rows(inputs, weights, split_at):
    both_parts = jnp.dot(inputs, weights, preferred_element_type=jnp.float32)
    return (jax.nn.silu(both_parts[:, :split_at]) * both_parts[:, split_at:]).astype(jnp.bfloat16)


def down_fold(down_matrix, hidden_piece):
    return jnp.dot(hidden_piece, down_matrix, preferred_element_type=jnp.float32)


def local(tokens, routes, gate_values, gate_up, down_weight):
    devices = lax.axis_size("expert")
    experts = devices // 2
    tok_count, choices = routes.shape
    features = tokens.shape[1]
    hidden_width = gate_up.shape[3]
    half_units = down_weight.shape[1]
    columns = down_weight.shape[2]
    capacity = capacity_of(tok_count, choices, experts)
    slot_rows = capacity // 2
    targets = experts * capacity
    expert_ids = routes.reshape(-1)
    member = (expert_ids[:, None] == jnp.arange(experts, dtype=jnp.int32)[None, :]).astype(
        jnp.int32
    )
    rows = jnp.arange(tok_count * choices, dtype=jnp.int32)
    before = (rows[None, :] < rows[:, None]).astype(jnp.bfloat16)
    ranks = jnp.dot(before, member.astype(jnp.bfloat16), preferred_element_type=jnp.float32)
    earlier = jnp.sum(ranks.astype(jnp.int32) * member, axis=1)
    target = expert_ids * capacity + earlier
    target_hot = (target[:, None] == jnp.arange(targets, dtype=jnp.int32)[None, :]).astype(
        jnp.bfloat16
    )
    repeated = jnp.broadcast_to(tokens[:, None, :], (tok_count, choices, features)).reshape(
        tok_count * choices, features
    )
    outgoing = lax.dot_general(
        target_hot, repeated, (((0,), (0,)), ((), ())), preferred_element_type=jnp.float32
    ).astype(jnp.bfloat16)
    own_half = lax.axis_index("expert") % 2
    doubled = jnp.broadcast_to(
        outgoing.reshape(experts, 1, capacity, features), (experts, 2, capacity, features)
    )
    arrived = lax.all_to_all(
        doubled.reshape(devices * capacity, features),
        "expert",
        split_axis=0,
        concat_axis=0,
        tiled=True,
    )
    own_gate_up = gate_up.reshape(features, 2 * hidden_width)
    own_down = down_weight.reshape(half_units, columns)
    hidden_all = swiglu_rows(arrived, own_gate_up, hidden_width)
    summed = down_fold(own_down, lax.all_gather(hidden_all, "hslice", axis=1, tiled=True))
    summed = summed.astype(jnp.bfloat16)
    partner = partner_2(summed, "expert", 0)
    pair_total = (
        (summed.astype(jnp.float32) + partner.astype(jnp.float32))
        .astype(jnp.bfloat16)
        .reshape(devices, 2, slot_rows, columns)
    )
    kept_slot = jnp.where(own_half == 0, pair_total[:, 0], pair_total[:, 1]).reshape(
        devices * slot_rows, columns
    )
    merged = lax.all_to_all(kept_slot, "expert", split_axis=0, concat_axis=0, tiled=True)
    merged = merged.astype(jnp.float32)
    weights_map = (target_hot.astype(jnp.float32) * gate_values.reshape(-1)[:, None]).reshape(
        tok_count, choices, targets
    )
    weights_map = jnp.sum(weights_map, axis=1)
    mixed_out = jnp.dot(
        weights_map, merged, precision=lax.Precision.HIGHEST, preferred_element_type=jnp.float32
    )
    return mixed_out.astype(jnp.bfloat16)


def local_any(tokens, routes, gate_values, gate_up, down_weight):
    devices = lax.axis_size("expert")
    tok, choices = routes.shape
    planes = devices // 8
    fits = (
        lax.axis_size("hslice") == 1
        and devices % 8 == 0
        and planes in (2, 4)
        and devices // 2 <= 128
        and tok % 16 == 0
        and planes * capacity_of(tok, choices, devices // 2) % 16 == 0
        and tokens.shape[1] % 128 == 0
        and gate_up.shape[3] % 128 == 0
    )
    call = fused if fits else local
    return call(tokens, routes, gate_values, gate_up, down_weight)


def solution(mesh):
    in_specs = (
        P(("group", "expert"), None),
        P(("group", "expert"), None),
        P(("group", "expert"), None),
        P("expert", None, None, "hslice"),
        P("expert", None, "hslice"),
    )
    out_specs = P(("group", "expert"), "hslice")
    return jax.shard_map(local_any, mesh=mesh, in_specs=in_specs, out_specs=out_specs, check_vma=False)
```

```python
import functools

import jax
import jax.numpy as jnp
from jax import lax
from jax.experimental import pallas as pl
from jax.experimental.pallas import tpu as pltpu
from jax.sharding import PartitionSpec as P

MESH = pl.DeviceIdType.MESH
F32 = jnp.float32
BF16 = jnp.bfloat16


def capacity_of(tok_count, choices, experts):
    return min(tok_count, 2 * ((9 * tok_count * choices + 16 * experts - 1) // (16 * experts)))


def chunks_of(features):
    for count in (7, 4, 2):
        if features % (count * 128) == 0:
            return count
    return 1


def fused_kernel(
    planes, cap, chunks,
    tokens, routes, gates, gate_up, down,
    out,
    info, line, pack_hot, mix_hi, mix_lo, rows_out, rows_in, acc, hidden,
    w_raw, w_up, w_down, y_out, y_in, part, part_own, part_in,
    i_s, i_r, z_s, z_r, x_s, x_r, y_s, y_r, p_s, p_r, wl, ws, wr, dl, ds, dr,
):
    me = lax.axis_index("expert")
    core = lax.rem(me, 2)
    x = lax.rem(me // 2, 2)
    y = lax.rem(me // 4, 2)
    z = me // 8
    tok = tokens.shape[0]
    width = tokens.shape[1] // chunks
    half = gate_up.shape[2]
    group = planes * cap
    partner = me + 1 - 2 * core

    def z_peer(d):
        return lax.rem(z + d, planes) * 8 + y * 4 + x * 2 + core

    def plane_xy(r):
        px = x if r % 2 == 0 else 1 - x
        py = y if r // 2 == 0 else 1 - y
        return py, px

    def xy_peer(r):
        py, px = plane_xy(r)
        return z * 8 + py * 4 + px * 2 + core

    def remote(src, dst, s, r, device):
        return pltpu.make_async_remote_copy(
            src_ref=src, dst_ref=dst, send_sem=s, recv_sem=r,
            device_id={"expert": device}, device_id_type=MESH)

    def columns(j):
        return pl.ds(pl.multiple_of(j * width, 128), width)

    own_rows = pl.ds(pl.multiple_of(z * tok, 16), tok)

    def up_local(j):
        return pltpu.make_async_copy(
            gate_up.at[pl.ds(j * width, width)], w_raw.at[pl.ds(j * width, width)], wl.at[j])

    def up_swap(j):
        return remote(w_up.at[0, :, pl.ds(j * width, width)],
                      w_up.at[1, :, pl.ds(j * width, width)], ws.at[j], wr.at[j], partner)

    down_local = pltpu.make_async_copy(down, w_down.at[pl.ds(0, half)], dl)
    down_swap = remote(down, w_down.at[pl.ds(half, half)], ds, dr, partner)

    def info_send(d):
        return remote(info.at[z], info.at[z], i_s.at[d - 1], i_r.at[d - 1], z_peer(d))

    def block_rows(block):
        return pl.ds(pl.multiple_of(block * tok, 16), tok)

    last = planes - 1
    sides = ((1, me + 8), (-1, me - 8))

    def z_copy(side, step, j, block):
        sign, peer = sides[side]
        k = side * last + step - 1
        where = line.at[j, block_rows(block)]
        return remote(where, where, z_s.at[k, j], z_r.at[k, j], peer)

    def inside(block):
        return jnp.logical_and(block >= 0, block <= last)

    def z_sending(side, step):
        sign, _ = sides[side]
        block = z - sign * (step - 1)
        return jnp.logical_and(inside(block), inside(z + sign)), block

    def z_start(step, j):
        for side in range(2):
            allowed, block = z_sending(side, step)

            @pl.when(allowed)
            def _():
                z_copy(side, step, j, block).start()

    def z_wait(step, j):
        for side in range(2):
            block = z - sides[side][0] * step

            @pl.when(inside(block))
            def _():
                z_copy(side, step, j, block).wait_recv()

    def x_send(r, j):
        return remote(rows_out.at[j, pl.ds((r - 1) * group, group)],
                      rows_in.at[j, pl.ds(r * group, group)],
                      x_s.at[r - 1, j], x_r.at[r - 1, j], xy_peer(r))

    def y_send(r, j):
        return remote(y_out.at[j, pl.ds((r - 1) * group, group)],
                      y_in.at[j, pl.ds(r * group, group)],
                      y_s.at[r - 1, j], y_r.at[r - 1, j], xy_peer(r))

    def p_send(d, j):
        there = pl.ds(pl.multiple_of(lax.rem(z + d, planes) * tok, 16), tok)
        return remote(part.at[j, there], part_in.at[j, d - 1],
                      p_s.at[d - 1, j], p_r.at[d - 1, j], z_peer(d))

    def each_chunk(body):
        def step(j, carry):
            body(j)
            return carry
        lax.fori_loop(0, chunks, step, 0)

    each_chunk(lambda j: up_local(j).start())
    down_local.start()

    expert_row = lax.broadcasted_iota(jnp.int32, (128, tok), 0)
    weight_t = jnp.zeros((128, tok), F32)
    for k in range(routes.shape[0]):
        weight_t = weight_t + jnp.where(routes[k:k + 1, :] == expert_row, gates[k:k + 1, :], 0.0)
    weight = jnp.transpose(weight_t)
    member = jnp.where(weight > 0.0, 1.0, 0.0)
    lower = jnp.where(
        lax.broadcasted_iota(jnp.int32, (tok, tok), 1) < lax.broadcasted_iota(jnp.int32, (tok, tok), 0),
        1.0, 0.0).astype(BF16)
    rank = jnp.dot(lower, member.astype(BF16), preferred_element_type=F32)
    slot = jnp.where(weight > 0.0, rank + (z * cap).astype(F32), -10000.0)
    info[z, :, 0:128] = weight
    info[z, :, 128:256] = slot

    barrier = pltpu.get_barrier_semaphore()
    peers = [z_peer(d) for d in range(1, planes)] + [xy_peer(r) for r in (1, 2, 3)] + [partner]
    for peer in peers:
        pl.semaphore_signal(barrier, inc=1, device_id={"expert": peer}, device_id_type=MESH)
    pl.semaphore_wait(barrier, len(peers))

    for d in range(1, planes):
        info_send(d).start()

    def own_line(j):
        line[j, own_rows, :] = tokens[:, columns(j)]
    each_chunk(own_line)
    ahead = min(2, chunks)
    for j in range(ahead):
        z_start(1, j)
    down_swap.start()

    for d in range(1, planes):
        info_send(d).wait_recv()

    total = planes * tok
    info_all = info[...].reshape(total, 256)
    weights = info_all[:, 0:128]
    slots = info_all[:, 128:256]
    slots_t = jnp.transpose(slots)
    row_id = lax.broadcasted_iota(jnp.int32, (128, total), 0)
    col_id = lax.broadcasted_iota(jnp.int32, (total, 128), 1)
    pack = jnp.zeros((4 * group, total), F32)
    mix = jnp.zeros((total, 4 * group), F32)
    pack_at = lax.broadcasted_iota(jnp.int32, (4 * group, total), 0).astype(F32)
    mix_at = lax.broadcasted_iota(jnp.int32, (total, 4 * group), 1).astype(F32)
    for r in range(4):
        py, px = plane_xy(r)
        expert = z * 4 + py * 2 + px
        slot_row = jnp.sum(jnp.where(row_id == expert, slots_t, 0.0), axis=0, keepdims=True)
        slot_col = jnp.sum(jnp.where(col_id == expert, slots, 0.0), axis=1, keepdims=True)
        weight_col = jnp.sum(jnp.where(col_id == expert, weights, 0.0), axis=1, keepdims=True)
        pack = pack + jnp.where(pack_at == slot_row + float(r * group), 1.0, 0.0)
        mix = mix + jnp.where(mix_at == slot_col + float(r * group), weight_col, 0.0)
    pack_hot[...] = pack.astype(BF16)
    high = mix.astype(BF16)
    mix_hi[...] = high
    mix_lo[...] = (mix - high.astype(F32)).astype(BF16)

    def pack_step(j):
        packed = jnp.dot(pack_hot[...], line[j], preferred_element_type=F32).astype(BF16)
        rows_out[j] = packed[group:]
        for r in (3, 1, 2):
            x_send(r, j).start()
        rows_in[j, 0:group, :] = packed[0:group]

        up_local(j).wait()

        def split(n, carry):
            rows = pl.ds(pl.multiple_of(j * width + n * 32, 32), 32)
            w_up[0, 0, rows, :] = w_raw[rows, 0, :]
            w_up[0, 1, rows, :] = w_raw[rows, 1, :]
            return carry
        lax.fori_loop(0, width // 32, split, 0)
        up_swap(j).start()

    def gather_step(i, carry):
        @pl.when(i + ahead < chunks)
        def _():
            z_start(1, i + ahead)
        for step in range(1, planes):
            j = i - (step - 1)

            @pl.when(jnp.logical_and(j >= 0, j < chunks))
            def _():
                z_wait(step, j)
                if step < last:
                    z_start(step + 1, j)
                else:
                    pack_step(j)
        return carry
    lax.fori_loop(0, chunks + planes - 2, gather_step, 0)

    def up_step(j):
        for r in (1, 2, 3):
            x_send(r, j).wait_recv()
        up_swap(j).wait_recv()

        def tile(n, carry):
            h, g = n // 2, lax.rem(n, 2)
            term = jnp.dot(rows_in[j], w_up[h, g, pl.ds(j * width, width), :],
                           preferred_element_type=F32)

            @pl.when(j == 0)
            def _():
                acc[n] = term

            @pl.when(j > 0)
            def _():
                acc[n] = acc[n] + term
            return carry
        lax.fori_loop(0, 4, tile, 0)
    each_chunk(up_step)

    for h in range(2):
        gate = acc[2 * h]
        hidden[:, h * half:(h + 1) * half] = (gate / (1.0 + jnp.exp(-gate)) * acc[2 * h + 1]).astype(BF16)

    down_local.wait()
    down_swap.wait_recv()

    def down_step(j):
        result = jnp.dot(hidden[...], w_down[:, columns(j)], preferred_element_type=F32).astype(BF16)
        y_out[j] = result[group:]
        for r in (3, 1, 2):
            y_send(r, j).start()
        y_in[j, 0:group, :] = result[0:group]
    each_chunk(down_step)

    def mix_step(j):
        for r in (1, 2, 3):
            y_send(r, j).wait_recv()
        rows = y_in[j]
        part_own[j] = (jnp.dot(mix_hi[...], rows, preferred_element_type=F32)
                       + jnp.dot(mix_lo[...], rows, preferred_element_type=F32))
        part[j] = part_own[j].astype(BF16)
        for d in range(1, planes):
            p_send(d, j).start()
    each_chunk(mix_step)

    def last_step(j):
        for d in range(1, planes):
            p_send(d, j).wait_recv()
        value = part_own[j, own_rows, :]
        for d in range(1, planes):
            value = value + part_in[j, d - 1].astype(F32)
        out[:, columns(j)] = value.astype(BF16)
    each_chunk(last_step)

    for d in range(1, planes):
        info_send(d).wait_send()

    def drain(j):
        for d in range(1, planes):
            for side in range(2):
                allowed, block = z_sending(side, d)

                @pl.when(allowed)
                def _():
                    z_copy(side, d, j, block).wait_send()
            p_send(d, j).wait_send()
        for r in (1, 2, 3):
            x_send(r, j).wait_send()
            y_send(r, j).wait_send()
        up_swap(j).wait_send()
    each_chunk(drain)
    down_swap.wait_send()


def fused(tokens, routes, gate_values, gate_up, down_weight):
    devices = lax.axis_size("expert")
    planes = devices // 8
    tok, choices = routes.shape
    features = tokens.shape[1]
    half = gate_up.shape[3]
    cap = capacity_of(tok, choices, devices // 2)
    chunks = chunks_of(features)
    width = features // chunks
    group = planes * cap
    total = planes * tok
    up = gate_up.reshape(features, 2, half)
    down = down_weight.reshape(half, features)
    dma = pltpu.SemaphoreType.DMA
    vmem = pltpu.VMEM
    pairs = lambda n: [dma((n, chunks)), dma((n, chunks))]
    return pl.pallas_call(
        functools.partial(fused_kernel, planes, cap, chunks),
        out_shape=jax.ShapeDtypeStruct((tok, features), BF16),
        in_specs=[pl.BlockSpec(memory_space=pltpu.VMEM)] * 3 + [pl.BlockSpec(memory_space=pl.ANY)] * 2,
        out_specs=pl.BlockSpec(memory_space=pltpu.VMEM),
        scratch_shapes=[
            vmem((planes, tok, 256), F32),
            vmem((chunks, total, width), BF16),
            vmem((4 * group, total), BF16),
            vmem((total, 4 * group), BF16),
            vmem((total, 4 * group), BF16),
            vmem((chunks, 3 * group, width), BF16),
            vmem((chunks, 4 * group, width), BF16),
            vmem((4, 4 * group, half), F32),
            vmem((4 * group, 2 * half), BF16),
            vmem((features, 2, half), BF16),
            vmem((2, 2, features, half), BF16),
            vmem((2 * half, features), BF16),
            vmem((chunks, 3 * group, width), BF16),
            vmem((chunks, 4 * group, width), BF16),
            vmem((chunks, total, width), BF16),
            vmem((chunks, total, width), F32),
            vmem((chunks, planes - 1, tok, width), BF16),
            dma((planes - 1,)), dma((planes - 1,)),
            *pairs(2 * (planes - 1)), *pairs(3), *pairs(3), *pairs(planes - 1),
            dma((chunks,)), dma((chunks,)), dma((chunks,)), dma, dma, dma,
        ],
        compiler_params=pltpu.CompilerParams(
            collective_id=0, has_side_effects=True, vmem_limit_bytes=62 * 1024 * 1024),
    )(tokens, jnp.transpose(routes), jnp.transpose(gate_values), up, down)


def partner_2(block, axis, distance):
    count = lax.axis_size(axis)
    route = []
    for low in range(count):
        high = low | 1 << distance
        if high != low and high < count:
            route += [(low, high), (high, low)]
    return lax.ppermute(block, axis, route)


def swiglu_rows(inputs, weights, split_at):
    both_parts = jnp.dot(inputs, weights, preferred_element_type=jnp.float32)
    return (jax.nn.silu(both_parts[:, :split_at]) * both_parts[:, split_at:]).astype(jnp.bfloat16)


def down_fold(down_matrix, hidden_piece):
    return jnp.dot(hidden_piece, down_matrix, preferred_element_type=jnp.float32)


def local(tokens, routes, gate_values, gate_up, down_weight):
    devices = lax.axis_size("expert")
    experts = devices // 2
    tok_count, choices = routes.shape
    features = tokens.shape[1]
    hidden_width = gate_up.shape[3]
    half_units = down_weight.shape[1]
    columns = down_weight.shape[2]
    capacity = capacity_of(tok_count, choices, experts)
    slot_rows = capacity // 2
    targets = experts * capacity
    expert_ids = routes.reshape(-1)
    member = (expert_ids[:, None] == jnp.arange(experts, dtype=jnp.int32)[None, :]).astype(
        jnp.int32
    )
    rows = jnp.arange(tok_count * choices, dtype=jnp.int32)
    before = (rows[None, :] < rows[:, None]).astype(jnp.bfloat16)
    ranks = jnp.dot(before, member.astype(jnp.bfloat16), preferred_element_type=jnp.float32)
    earlier = jnp.sum(ranks.astype(jnp.int32) * member, axis=1)
    target = expert_ids * capacity + earlier
    target_hot = (target[:, None] == jnp.arange(targets, dtype=jnp.int32)[None, :]).astype(
        jnp.bfloat16
    )
    repeated = jnp.broadcast_to(tokens[:, None, :], (tok_count, choices, features)).reshape(
        tok_count * choices, features
    )
    outgoing = lax.dot_general(
        target_hot, repeated, (((0,), (0,)), ((), ())), preferred_element_type=jnp.float32
    ).astype(jnp.bfloat16)
    own_half = lax.axis_index("expert") % 2
    doubled = jnp.broadcast_to(
        outgoing.reshape(experts, 1, capacity, features), (experts, 2, capacity, features)
    )
    arrived = lax.all_to_all(
        doubled.reshape(devices * capacity, features),
        "expert",
        split_axis=0,
        concat_axis=0,
        tiled=True,
    )
    own_gate_up = gate_up.reshape(features, 2 * hidden_width)
    own_down = down_weight.reshape(half_units, columns)
    hidden_all = swiglu_rows(arrived, own_gate_up, hidden_width)
    summed = down_fold(own_down, lax.all_gather(hidden_all, "hslice", axis=1, tiled=True))
    summed = summed.astype(jnp.bfloat16)
    partner = partner_2(summed, "expert", 0)
    pair_total = (
        (summed.astype(jnp.float32) + partner.astype(jnp.float32))
        .astype(jnp.bfloat16)
        .reshape(devices, 2, slot_rows, columns)
    )
    kept_slot = jnp.where(own_half == 0, pair_total[:, 0], pair_total[:, 1]).reshape(
        devices * slot_rows, columns
    )
    merged = lax.all_to_all(kept_slot, "expert", split_axis=0, concat_axis=0, tiled=True)
    merged = merged.astype(jnp.float32)
    weights_map = (target_hot.astype(jnp.float32) * gate_values.reshape(-1)[:, None]).reshape(
        tok_count, choices, targets
    )
    weights_map = jnp.sum(weights_map, axis=1)
    mixed_out = jnp.dot(
        weights_map, merged, precision=lax.Precision.HIGHEST, preferred_element_type=jnp.float32
    )
    return mixed_out.astype(jnp.bfloat16)


def local_any(tokens, routes, gate_values, gate_up, down_weight):
    devices = lax.axis_size("expert")
    tok, choices = routes.shape
    planes = devices // 8
    fits = (
        lax.axis_size("hslice") == 1
        and devices % 8 == 0
        and planes in (2, 4)
        and devices // 2 <= 128
        and tok % 16 == 0
        and planes * capacity_of(tok, choices, devices // 2) % 16 == 0
        and tokens.shape[1] % 128 == 0
        and gate_up.shape[3] % 128 == 0
    )
    call = fused if fits else local
    return call(tokens, routes, gate_values, gate_up, down_weight)


def solution(mesh):
    in_specs = (
        P(("group", "expert"), None),
        P(("group", "expert"), None),
        P(("group", "expert"), None),
        P("expert", None, None, "hslice"),
        P("expert", None, "hslice"),
    )
    out_specs = P(("group", "expert"), "hslice")
    return jax.shard_map(local_any, mesh=mesh, in_specs=in_specs, out_specs=out_specs, check_vma=False)
```
